32 devices in a mesh: row: 8 (over y, x, core), col: 4 (over z).
Axes of the slice: x: 2, y: 2, z: 4, core: 2. Of those that a mesh axis runs over, the one named last changes fastest.
Arguments:
- hidden: bfloat16 [2048, 14336], P('col', 'row'), may hold values from -6 to 6
- grad_out: bfloat16 [2048, 8192], P('row', 'col'), may hold values from -6 to 6
- weight_blocks: bfloat16 [8, 1792, 4096], P('row', 'col'), may hold values from -0.09375 to 0.09375
- block_index: int32 [8, 1792], P('row', 'col'), may hold values from 0 to 895, as said below
- block_count: int32 [8, 4], P('row', 'col'), may hold values from 1 to 448, as said below
Outputs:
- output: bfloat16 [2048, 8192], P('row', 'col')
- input_grad: bfloat16 [2048, 14336], P('col', 'row')
- weight_grad: bfloat16 [8, 1792, 4096], P('row', 'col')
The draws below stay inside these ranges and needn't reach their ends.
Inputs may be any that keep to these rules, and one draw needn't show every extreme that they name: `block_index`: within one tile the 448 entries are different block positions; slots at or past the tile's block_count are unused. `block_count`: live slots fill each tile from slot 0; some tile is full in every draw.
All inputs are finite; a program needn't handle non-finite values.
Results may differ from the reference program's by a relative error of at most 0.012.
Values may be sent and summed in bfloat16 or wider, within the bound.
A program may use at most 192 MiB of HBM per device.

```python
import math
import jax
import jax.numpy as jnp
from jax import lax

D = 8192
FF = 14336
BLOCK = 64
TOKENS = 2048
TILE = 896
CAP = 448
N_ROW = 8
N_COL = 4


def one_order(single):
    return jax.random.permutation(single, TILE)


def draw_block_index(key, part):
    key = jax.random.fold_in(key, 3)
    keys = jax.random.split(key, N_ROW * N_COL)
    orders = jax.vmap(one_order)(keys)
    return orders[:, :CAP].reshape(N_ROW, N_COL * CAP).astype(jnp.int32)


def draw_block_count(key, part):
    key = jax.random.fold_in(key, 5)
    counts = jax.random.randint(jax.random.fold_in(key, 1), (N_ROW * N_COL,), 1, CAP + 1)
    busiest = jax.random.randint(jax.random.fold_in(key, 2), (), 0, N_ROW * N_COL)
    counts = jnp.where(jnp.arange(N_ROW * N_COL) == busiest, CAP, counts)
    return counts.reshape(N_ROW, N_COL).astype(jnp.int32)


def level_of(stream_key, shape, cuts, low, top_value):
    def one(position, shards_of):
        steps = jax.random.uniform(jax.random.fold_in(jax.random.fold_in(stream_key, 6), position), (shards_of,), jnp.float32, low / len(cuts), top_value / len(cuts))
        return jnp.repeat(jnp.exp(steps), shape[position] // shards_of).reshape((-1,) + (1,) * (len(shape) - position - 1))

    level = one(*cuts[0])
    for cut in cuts[1:]:
        level = level * one(*cut)
    return level


def normal_values(own_key, dims, deviation, reach, pieces=(), held_as=jnp.bfloat16):
    values = jax.random.normal(own_key, dims, jnp.float32) * deviation
    if len(pieces) > 0:
        values = level_of(own_key, dims, pieces, -0.22, 0.18) * values
    return jnp.clip(values, min=-reach, max=reach).astype(held_as)


def setup_inputs(seed: int = 0) -> dict:
    splits = jax.random.split(jax.random.key(seed), 6)
    return {
        "hidden": normal_values(splits[0], (TOKENS, FF), 1.0, 6.0, ((0, 4), (1, 8))),
        "grad_out": normal_values(splits[1], (TOKENS, D), 1.0, 6.0, ((0, 8), (1, 4))),
        "weight_blocks": normal_values(splits[2], (N_ROW, N_COL * CAP, BLOCK * BLOCK), (FF // 4) ** -0.5, 0.09375, ((0, 8), (1, 4))),
        "block_index": draw_block_index(jax.random.fold_in(splits[5], 71), 0),
        "block_count": draw_block_count(jax.random.fold_in(splits[5], 71), 0),
    }


def dense_tile(slots, index, live, row_blocks, col_blocks):
    positions = jnp.arange(row_blocks * col_blocks, dtype=jnp.int32)
    onehot = ((positions[:, None] == index[None, :]) & live[None, :]).astype(jnp.bfloat16)
    flat = jnp.dot(onehot, slots, preferred_element_type=jnp.float32).astype(jnp.bfloat16)
    return flat.reshape(row_blocks, col_blocks, BLOCK, BLOCK).transpose(0, 2, 1, 3).reshape(row_blocks * BLOCK, col_blocks * BLOCK)

def reference(hidden, grad_out, weight_blocks, block_index, block_count):
    tile_rows = FF // N_ROW
    tile_cols = D // N_COL
    row_blocks = tile_rows // BLOCK
    col_blocks = tile_cols // BLOCK
    capacity = block_index.shape[1] // N_COL
    factor = 1.0 / math.sqrt(TOKENS)
    zero = jnp.zeros((), jnp.int32)

    def visit(carry, which):
        output_sum, input_sum = carry
        band = (which // N_COL).astype(jnp.int32)
        column = (which % N_COL).astype(jnp.int32)
        slots = lax.dynamic_slice(weight_blocks, (band, column * capacity, zero), (1, capacity, BLOCK * BLOCK))[0]
        index = lax.dynamic_slice(block_index, (band, column * capacity), (1, capacity))[0]
        filled = lax.dynamic_slice(block_count, (band, column), (1, 1))[0, 0]
        live = jnp.arange(capacity, dtype=jnp.int32) < filled
        tile = dense_tile(slots, index, live, row_blocks, col_blocks)
        h_band = lax.dynamic_slice_in_dim(hidden, band * tile_rows, tile_rows, 1)
        g_band = lax.dynamic_slice_in_dim(grad_out, column * tile_cols, tile_cols, 1)
        out_part = jnp.dot(h_band, tile, preferred_element_type=jnp.float32).astype(jnp.bfloat16)
        in_part = lax.dot_general(g_band, tile, (((1,), (1,)), ((), ())), preferred_element_type=jnp.float32).astype(jnp.bfloat16)
        out_part, in_part = lax.optimization_barrier((out_part, in_part))
        old_out = lax.dynamic_slice_in_dim(output_sum, column * tile_cols, tile_cols, 1)
        output_sum = lax.dynamic_update_slice_in_dim(output_sum, old_out + out_part.astype(jnp.float32), column * tile_cols, 1)
        old_in = lax.dynamic_slice_in_dim(input_sum, band * tile_rows, tile_rows, 1)
        input_sum = lax.dynamic_update_slice_in_dim(input_sum, old_in + in_part.astype(jnp.float32), band * tile_rows, 1)
        wide = lax.dot_general(h_band, g_band, (((0,), (0,)), ((), ())), preferred_element_type=jnp.float32) * factor
        blocks = wide.reshape(row_blocks, BLOCK, col_blocks, BLOCK).transpose(0, 2, 1, 3).reshape(row_blocks * col_blocks, BLOCK * BLOCK)
        picked = jnp.take(blocks, index, axis=0) * live[:, None].astype(jnp.float32)
        return ((output_sum, input_sum), picked.astype(jnp.bfloat16))
    start = (jnp.zeros((TOKENS, D), jnp.float32), jnp.zeros((TOKENS, FF), jnp.float32))
    (output_sum, input_sum), slot_grads = lax.scan(visit, start, jnp.arange(N_ROW * N_COL, dtype=jnp.int32))
    weight_grad = slot_grads.reshape(N_ROW, N_COL * capacity, BLOCK * BLOCK)
    return (output_sum.astype(jnp.bfloat16), input_sum.astype(jnp.bfloat16), weight_grad)
```

```python
import math

import jax
import jax.numpy as jnp
from jax import lax
from jax.experimental import pallas as pl
from jax.experimental.pallas import tpu as pltpu
from jax.sharding import PartitionSpec as P

BLOCK = 64
UNROLL = 4
CORE, X, Y = 1, 2, 4


def dense_tile(slots, index, live, row_blocks, col_blocks):
    positions = jnp.arange(row_blocks * col_blocks, dtype=jnp.int32)
    onehot = ((positions[:, None] == index[None, :]) & live[None, :]).astype(jnp.bfloat16)
    flat = jnp.dot(onehot, slots, preferred_element_type=jnp.float32).astype(jnp.bfloat16)
    return (
        flat.reshape(row_blocks, col_blocks, BLOCK, BLOCK)
        .transpose(0, 2, 1, 3)
        .reshape(row_blocks * BLOCK, col_blocks * BLOCK)
    )


def pick_kernel(col_blocks, capacity, index_ref, count_ref, wide_ref, out_ref, pair_ref):
    half = BLOCK // 2
    lane = lax.broadcasted_iota(jnp.int32, (half, 2 * BLOCK), 1)
    count = count_ref[0]

    def step(i, carry):
        for u in range(UNROLL):
            s = i * UNROLL + u
            k = index_ref[s]
            top = pl.multiple_of((k // col_blocks) * BLOCK, BLOCK)
            col = k % col_blocks
            left = pl.multiple_of((col // 2) * (2 * BLOCK), 2 * BLOCK)
            pair_ref[u] = wide_ref[pl.ds(top, BLOCK), pl.ds(left, 2 * BLOCK)]
            even = pair_ref[u, pl.ds(0, half, stride=2), :]
            odd = pair_ref[u, pl.ds(1, half, stride=2), :]
            first = jnp.where(lane < BLOCK, even, pltpu.roll(odd, BLOCK, 1))
            second = jnp.where(lane < BLOCK, pltpu.roll(even, BLOCK, 1), odd)
            block = jnp.where(col % 2 == 0, first, second)
            out_ref[s] = jnp.where(s < count, block, 0.0).astype(jnp.bfloat16)
        return carry

    lax.fori_loop(0, capacity // UNROLL, step, 0)


def pick_blocks(wide, index, count, col_blocks):
    capacity = index.shape[0]
    out = pl.pallas_call(
        lambda *refs: pick_kernel(col_blocks, capacity, *refs),
        out_shape=jax.ShapeDtypeStruct((capacity, BLOCK // 2, 2 * BLOCK), jnp.bfloat16),
        in_specs=[
            pl.BlockSpec(memory_space=pltpu.SMEM),
            pl.BlockSpec(memory_space=pltpu.SMEM),
            pl.BlockSpec(memory_space=pltpu.VMEM),
        ],
        out_specs=pl.BlockSpec(memory_space=pltpu.VMEM),
        scratch_shapes=[pltpu.VMEM((UNROLL, BLOCK, 2 * BLOCK), jnp.float32)],
        compiler_params=pltpu.CompilerParams(vmem_limit_bytes=40 * 1024 * 1024),
        cost_estimate=pl.CostEstimate(
            flops=0, bytes_accessed=3 * wide.size * 4, transcendentals=0
        ),
    )(index, count, wide)
    return out.reshape(capacity, BLOCK * BLOCK)


def swap(x, mask):
    return lax.ppermute(x, "row", [(r, r ^ mask) for r in range(8)])


def gather_row(g):
    me = lax.axis_index("row")
    half = g.shape[0] // 2
    gx, gy = swap(g, X), swap(g, Y)
    first = swap(gx[:half], Y)
    last = swap(gy[half:], X)
    mine = {0: g, X: gx, Y: gy}
    parts = [(m, 0, p) for m, p in mine.items()]
    parts += [(m ^ CORE, 0, swap(p, CORE)) for m, p in mine.items()]
    parts += [(X ^ Y, 0, first), (X ^ Y, half, last)]
    parts += [(X ^ Y ^ CORE, 0, swap(first, CORE)), (X ^ Y ^ CORE, half, swap(last, CORE))]
    whole = jnp.zeros((8 * g.shape[0], g.shape[1]), g.dtype)
    for m, start, p in parts:
        whole = lax.dynamic_update_slice(whole, p, ((me ^ m) * g.shape[0] + start, 0))
    return whole


def pick(x, i, axis):
    return lax.dynamic_index_in_dim(x, i, axis, keepdims=False)


def project_scatter_row(h_all, tile):
    me = lax.axis_index("row")
    core, x, y = me & 1, (me >> 1) & 1, (me >> 2) & 1
    share = h_all.shape[0] // 8
    split = h_all.reshape(4, 2, share, h_all.shape[1])
    width = tile.shape[1]
    mid = width // 2

    def product(which):
        rows = pick(split, which, 1).reshape(4 * share, -1)
        return jnp.dot(rows, tile, preferred_element_type=jnp.float32).astype(jnp.bfloat16)

    got = swap(product(1 - core), CORE)
    total = product(core).astype(jnp.float32) + got.astype(jnp.float32)
    total = total.astype(jnp.bfloat16).reshape(2, 2, share, width)
    a, b = total[..., :mid], total[..., mid:]

    def fold(v, axis, bit, mask):
        got = swap(pick(v, 1 - bit, axis), mask)
        return (pick(v, bit, axis).astype(jnp.float32) + got.astype(jnp.float32)).astype(
            jnp.bfloat16
        )

    a = fold(a, 1, x, X)
    b = fold(b, 0, y, Y)
    a = fold(a, 0, y, Y)
    b = fold(b, 0, x, X)
    return jnp.concatenate([a, b], axis=-1)


def body(small, hidden, grad_out, weight_blocks, block_index, block_count):
    row_blocks = hidden.shape[1] // BLOCK
    col_blocks = grad_out.shape[1] // BLOCK
    slots = weight_blocks[0]
    index = block_index[0]
    filled = block_count[0, 0]
    capacity = slots.shape[0]
    live = jnp.arange(capacity, dtype=jnp.int32) < filled
    h_all = lax.all_gather(hidden, "col", axis=0, tiled=True)
    if small:
        g_all = gather_row(grad_out)
    else:
        g_all = lax.all_gather(grad_out, "row", axis=0, tiled=True)
    tokens = h_all.shape[0]
    factor = 1.0 / math.sqrt(tokens)
    tile = dense_tile(slots, index, live, row_blocks, col_blocks)
    input_grad = lax.psum_scatter(
        lax.dot_general(
            g_all, tile, (((1,), (1,)), ((), ())), preferred_element_type=jnp.float32
        ).astype(jnp.bfloat16),
        "col",
        scatter_dimension=0,
        tiled=True,
    )
    if small:
        output = project_scatter_row(h_all, tile)
    else:
        output = lax.psum_scatter(
            jnp.dot(h_all, tile, preferred_element_type=jnp.float32).astype(jnp.bfloat16),
            "row",
            scatter_dimension=0,
            tiled=True,
        )
    wide = (
        lax.dot_general(h_all, g_all, (((0,), (0,)), ((), ())), preferred_element_type=jnp.float32)
        * factor
    )
    slot_grads = pick_blocks(wide, index, block_count[0], col_blocks)
    return (output, input_grad, slot_grads[None])


def solution(mesh):
    small = mesh.shape["row"] == 8

    def local(*args):
        return body(small, *args)

    return jax.shard_map(
        local,
        mesh=mesh,
        in_specs=(
            P("col", "row"),
            P("row", "col"),
            P("row", "col", None),
            P("row", "col"),
            P("row", "col"),
        ),
        out_specs=(P("row", "col"), P("col", "row"), P("row", "col", None)),
        check_vma=False,
    )
```

```python
import math

import jax
import jax.numpy as jnp
from jax import lax
from jax.experimental import pallas as pl
from jax.experimental.pallas import tpu as pltpu
from jax.sharding import PartitionSpec as P

BLOCK = 64
UNROLL = 7
CORE, X, Y = 1, 2, 4


def pick_kernel(col_blocks, capacity, index_ref, count_ref, wide_ref, out_ref, pair_ref):
    half = BLOCK // 2
    lane = lax.broadcasted_iota(jnp.int32, (half, 2 * BLOCK), 1)
    count = count_ref[0]

    def step(i, carry):
        for u in range(UNROLL):
            s = i * UNROLL + u
            k = index_ref[s]
            top = pl.multiple_of((k // col_blocks) * BLOCK, BLOCK)
            col = k % col_blocks
            left = pl.multiple_of((col // 2) * (2 * BLOCK), 2 * BLOCK)
            pair_ref[u] = wide_ref[pl.ds(top, BLOCK), pl.ds(left, 2 * BLOCK)]
            even = pair_ref[u, pl.ds(0, half, stride=2), :]
            odd = pair_ref[u, pl.ds(1, half, stride=2), :]
            first = jnp.where(lane < BLOCK, even, pltpu.roll(odd, BLOCK, 1))
            second = jnp.where(lane < BLOCK, pltpu.roll(even, BLOCK, 1), odd)
            block = jnp.where(col % 2 == 0, first, second)
            out_ref[s] = jnp.where(s < count, block, 0.0).astype(jnp.bfloat16)
        return carry

    lax.fori_loop(0, capacity // UNROLL, step, 0)


def build_kernel(col_blocks, capacity, index_ref, count_ref, slot_ref, tile_ref, pair_ref):
    half = BLOCK // 2
    lane = lax.broadcasted_iota(jnp.int32, (half, 2 * BLOCK), 1)
    side = lax.broadcasted_iota(jnp.int32, (BLOCK, 2 * BLOCK), 1) // BLOCK
    count = count_ref[0]

    def clear(i, carry):
        top = pl.multiple_of(i * BLOCK, BLOCK)
        tile_ref[pl.ds(top, BLOCK), :] = jnp.zeros((BLOCK, tile_ref.shape[1]), tile_ref.dtype)
        return carry

    lax.fori_loop(0, tile_ref.shape[0] // BLOCK, clear, 0)

    def step(i, carry):
        for u in range(UNROLL):
            s = i * UNROLL + u
            k = index_ref[s]
            top = pl.multiple_of((k // col_blocks) * BLOCK, BLOCK)
            col = k % col_blocks
            left = pl.multiple_of((col // 2) * (2 * BLOCK), 2 * BLOCK)
            v = slot_ref[s].astype(jnp.float32)
            turned = pltpu.roll(v, BLOCK, 1)
            pair_ref[u, pl.ds(0, half, stride=2), :] = jnp.where(lane < BLOCK, v, turned)
            pair_ref[u, pl.ds(1, half, stride=2), :] = jnp.where(lane < BLOCK, turned, v)
            place = (pl.ds(top, BLOCK), pl.ds(left, 2 * BLOCK))
            want = jnp.where(s < count, col % 2, 2)
            old = tile_ref[place].astype(jnp.float32)
            tile_ref[place] = jnp.where(side == want, pair_ref[u], old).astype(jnp.bfloat16)
        return carry

    lax.fori_loop(0, capacity // UNROLL, step, 0)


def build_tile(slots, index, count, row_blocks, col_blocks):
    capacity = index.shape[0]
    return pl.pallas_call(
        lambda *refs: build_kernel(col_blocks, capacity, *refs),
        out_shape=jax.ShapeDtypeStruct((row_blocks * BLOCK, col_blocks * BLOCK), jnp.bfloat16),
        in_specs=[
            pl.BlockSpec(memory_space=pltpu.SMEM),
            pl.BlockSpec(memory_space=pltpu.SMEM),
            pl.BlockSpec(memory_space=pltpu.VMEM),
        ],
        out_specs=pl.BlockSpec(memory_space=pltpu.VMEM),
        scratch_shapes=[pltpu.VMEM((UNROLL, BLOCK, 2 * BLOCK), jnp.float32)],
        compiler_params=pltpu.CompilerParams(vmem_limit_bytes=40 * 1024 * 1024),
        cost_estimate=pl.CostEstimate(
            flops=0, bytes_accessed=16 * slots.size, transcendentals=0
        ),
    )(index, count, slots.reshape(capacity, BLOCK // 2, 2 * BLOCK))


def pick_blocks(wide, index, count, col_blocks):
    capacity = index.shape[0]
    out = pl.pallas_call(
        lambda *refs: pick_kernel(col_blocks, capacity, *refs),
        out_shape=jax.ShapeDtypeStruct((capacity, BLOCK // 2, 2 * BLOCK), jnp.bfloat16),
        in_specs=[
            pl.BlockSpec(memory_space=pltpu.SMEM),
            pl.BlockSpec(memory_space=pltpu.SMEM),
            pl.BlockSpec(memory_space=pltpu.VMEM),
        ],
        out_specs=pl.BlockSpec(memory_space=pltpu.VMEM),
        scratch_shapes=[pltpu.VMEM((UNROLL, BLOCK, 2 * BLOCK), jnp.float32)],
        compiler_params=pltpu.CompilerParams(vmem_limit_bytes=40 * 1024 * 1024),
        cost_estimate=pl.CostEstimate(
            flops=0, bytes_accessed=3 * wide.size * 4, transcendentals=0
        ),
    )(index, count, wide)
    return out.reshape(capacity, BLOCK * BLOCK)


def swap(x, mask):
    return lax.ppermute(x, "row", [(r, r ^ mask) for r in range(8)])


def gather_both(hidden, g, tile):
    me, z = lax.axis_index("row"), lax.axis_index("col")
    half = g.shape[0] // 2
    gx, gy = swap(g, X), swap(g, Y)
    up1 = shift(hidden, 1, 1)
    down1 = shift(hidden, -1, 1)
    other = swap(g, CORE)
    gx, gy, tile = lax.optimization_barrier((gx, gy, tile))
    first = swap(gx[:half], Y)
    last = swap(gy[half:], X)
    parts = [(0, 0, g), (X, 0, gx), (Y, 0, gy), (CORE, 0, other)]
    parts += [(X ^ CORE, 0, swap(gx, CORE)), (Y ^ CORE, 0, swap(gy, CORE))]
    first, last, up1, down1 = lax.optimization_barrier((first, last, up1, down1))
    up2 = shift(up1, 1, 2)
    down2 = shift(down1, -1, 2)
    parts += [(X ^ Y, 0, first), (X ^ Y, half, last)]
    parts += [(X ^ Y ^ CORE, 0, swap(first, CORE)), (X ^ Y ^ CORE, half, swap(last, CORE))]
    g_all = jnp.zeros((8 * g.shape[0], g.shape[1]), g.dtype)
    for m, start, p in parts:
        g_all = lax.dynamic_update_slice(g_all, p, ((me ^ m) * g.shape[0] + start, 0))
    in_part = input_product(g_all, tile)
    in_part, up2, down2 = lax.optimization_barrier((in_part, up2, down2))
    up3 = shift(up2, 1, 3)
    down3 = shift(down2, -1, 3)
    rows = hidden.shape[0]
    h_all = jnp.zeros((4 * rows, hidden.shape[1]), hidden.dtype)
    shards = [hidden]
    for k, (up, down) in enumerate(((up1, down3), (up2, down2), (up3, down1)), 1):
        shards.append(jnp.where(z >= k, up, down))
    for k, p in enumerate(shards):
        h_all = lax.dynamic_update_slice(h_all, p, (((z - k) & 3) * rows, 0))
    return h_all, g_all, tile, in_part


def shift(x, way, step):
    if way > 0:
        pairs = [(i, i + 1) for i in range(step - 1, 3)]
    else:
        pairs = [(i, i - 1) for i in range(4 - step, 0, -1)]
    return lax.ppermute(x, "col", pairs)


def input_product(g_all, tile):
    return lax.dot_general(
        g_all, tile, (((1,), (1,)), ((), ())), preferred_element_type=jnp.float32
    ).astype(jnp.bfloat16)


def pick(x, i, axis):
    return lax.dynamic_index_in_dim(x, i, axis, keepdims=False)


def project_scatter_row(h_all, tile):
    me = lax.axis_index("row")
    core, x, y = me & 1, (me >> 1) & 1, (me >> 2) & 1
    share = h_all.shape[0] // 8
    split = h_all.reshape(4, 2, share, h_all.shape[1])
    width = tile.shape[1]
    mid = width // 2

    def product(which):
        rows = pick(split, which, 1).reshape(4 * share, -1)
        return jnp.dot(rows, tile, preferred_element_type=jnp.float32).astype(jnp.bfloat16)

    got = swap(product(1 - core), CORE)
    total = product(core).astype(jnp.float32) + got.astype(jnp.float32)
    total = total.astype(jnp.bfloat16).reshape(2, 2, share, width)
    a, b = total[..., :mid], total[..., mid:]

    def fold(v, axis, bit, mask):
        got = swap(pick(v, 1 - bit, axis), mask)
        return (pick(v, bit, axis).astype(jnp.float32) + got.astype(jnp.float32)).astype(
            jnp.bfloat16
        )

    a = fold(a, 1, x, X)
    b = fold(b, 0, y, Y)
    a = fold(a, 0, y, Y)
    b = fold(b, 0, x, X)
    return jnp.concatenate([a, b], axis=-1)


def body(small, hidden, grad_out, weight_blocks, block_index, block_count):
    row_blocks = hidden.shape[1] // BLOCK
    col_blocks = grad_out.shape[1] // BLOCK
    slots = weight_blocks[0]
    index = block_index[0]
    tile = build_tile(slots, index, block_count[0], row_blocks, col_blocks)
    if small:
        h_all, g_all, tile, in_part = gather_both(hidden, grad_out, tile)
    else:
        h_all = lax.all_gather(hidden, "col", axis=0, tiled=True)
        g_all = lax.all_gather(grad_out, "row", axis=0, tiled=True)
        in_part = input_product(g_all, tile)
    tokens = h_all.shape[0]
    factor = 1.0 / math.sqrt(tokens)
    input_grad = lax.psum_scatter(in_part, "col", scatter_dimension=0, tiled=True)
    if small:
        output = project_scatter_row(h_all, tile)
    else:
        output = lax.psum_scatter(
            jnp.dot(h_all, tile, preferred_element_type=jnp.float32).astype(jnp.bfloat16),
            "row",
            scatter_dimension=0,
            tiled=True,
        )
    wide = (
        lax.dot_general(h_all, g_all, (((0,), (0,)), ((), ())), preferred_element_type=jnp.float32)
        * factor
    )
    slot_grads = pick_blocks(wide, index, block_count[0], col_blocks)
    return (output, input_grad, slot_grads[None])


def solution(mesh):
    small = mesh.shape["row"] == 8 and mesh.shape["col"] == 4

    def local(*args):
        return body(small, *args)

    return jax.shard_map(
        local,
        mesh=mesh,
        in_specs=(
            P("col", "row"),
            P("row", "col"),
            P("row", "col", None),
            P("row", "col"),
            P("row", "col"),
        ),
        out_specs=(P("row", "col"), P("col", "row"), P("row", "col", None)),
        check_vma=False,
    )
```
